32 devices in a mesh: rep: 2 (over y), seq: 4 (over z), head: 4 (over x, core).
Axes of the slice: x: 2, y: 2, z: 4, core: 2. Of those that a mesh axis runs over, the one named last changes fastest.
Arguments:
- query: bfloat16 [4096, 4096], P(('rep', 'seq', 'head')), parts along dimension 0, may hold values from -0.25 to 0.25
- keys: bfloat16 [4096, 4096], P(('rep', 'seq', 'head')), parts along dimension 0, may hold values from -0.25 to 0.25
- values: bfloat16 [4096, 4096], P(('rep', 'seq', 'head')), parts along dimension 0, may hold values from -0.25 to 0.25
- grad_out: bfloat16 [4096, 4096], P(('rep', 'seq', 'head')), parts along dimension 0, may hold values from -6 to 6
Outputs:
- grad_query: bfloat16 [4096, 4096], P(('rep', 'seq', 'head')), parts along dimension 0
- grad_keys: bfloat16 [4096, 4096], P(('rep', 'seq', 'head')), parts along dimension 0
- grad_values: bfloat16 [4096, 4096], P(('rep', 'seq', 'head')), parts along dimension 0
The draws below stay inside these ranges and needn't reach their ends.
There are 2 independent parts, one for each index of `rep`. The reference program is written for one: setup_inputs(seed, part) draws one part's arguments, and reference() takes and returns one part's arrays. A program takes and returns all parts, laid end to end along the dimension named above; each array names one. Nothing has to cross between parts.
All inputs are finite; a program needn't handle non-finite values.
Results may differ from the reference program's by a relative error of at most 0.0032.
Values may be sent and summed in bfloat16 or wider, within the bound.
A program may use at most 128 MiB of HBM per device.

```python
import jax
import jax.numpy as jnp
from jax import lax

HEADS = 32
HD = 128
TOK_DEV = 128
SEQLEN = 2048
D = 4096


def levels(key, extent, cuts, smallest, top_value):
    def one(position, blocks):
        draws = jax.random.uniform(jax.random.fold_in(jax.random.fold_in(key, 6), position), (blocks,), jnp.float32, smallest / len(cuts), top_value / len(cuts))
        return jnp.repeat(jnp.exp(draws), extent[position] // blocks).reshape((-1,) + (1,) * (len(extent) - position - 1))

    level = one(*cuts[0])
    for cut in cuts[1:]:
        level = level * one(*cut)
    return level


def normal_values(rng, dims, width, most, cuts=(), kind=jnp.bfloat16):
    level = levels(rng, dims, cuts, -0.22, 0.18) if cuts else 1.0
    values = jax.random.normal(rng, dims, jnp.float32) * width * level
    return jnp.minimum(jnp.maximum(values, -most), most).astype(kind)


def setup_inputs(seed: int = 0, part: int = 0) -> dict:
    seeds = jax.random.split(jax.random.key(seed), 5)
    part_keys = jax.random.split(jax.random.fold_in(seeds[4], part), 5)
    return {
        "query": normal_values(part_keys[0], (SEQLEN, D), ((SEQLEN * HD) ** -0.25), 0.25, ((0, 16),)),
        "keys": normal_values(part_keys[1], (SEQLEN, D), ((SEQLEN * HD) ** -0.25), 0.25, ((0, 16),)),
        "values": normal_values(part_keys[2], (SEQLEN, D), ((SEQLEN * HD) ** -0.25), 0.25, ((0, 16),)),
        "grad_out": normal_values(part_keys[3], (SEQLEN, D), 1.0, 6.0, ((0, 16),)),
    }


def reference(query, keys, values, grad_out):
    block = 4 * TOK_DEV
    nblocks = SEQLEN // block
    highest = lax.Precision.HIGHEST
    causal = jnp.arange(block)[:, None] >= jnp.arange(block)[None, :]

    def split(array):
        return array.astype(jnp.float32).reshape(nblocks, block, HEADS, HD).transpose(0, 2, 1, 3)

    def scores(left, right):
        full = jnp.einsum("hti,hsi->hts", left, right, precision=highest)
        masked = jnp.where(causal[None], full, 0.0).astype(jnp.bfloat16)
        return lax.optimization_barrier(masked).astype(jnp.float32)

    query_b, keys_b, values_b, grad_b = split(query), split(keys), split(values), split(grad_out)
    empty_state = jnp.zeros((HEADS, HD, HD), jnp.float32)

    def forward(state, pieces):
        query_p, keys_p, values_p, grad_p = pieces
        out_score = scores(grad_p, values_p)
        grad_q = jnp.einsum("hts,hsi->hti", out_score, keys_p, precision=highest)
        grad_q = grad_q + jnp.einsum("htj,hij->hti", grad_p, state, precision=highest)
        state = state + jnp.einsum("hsi,hsj->hij", keys_p, values_p, precision=highest)
        return state, grad_q

    def backward(state, pieces):
        query_p, keys_p, values_p, grad_p = pieces
        out_score = scores(grad_p, values_p)
        key_score = scores(query_p, keys_p)
        grad_k = jnp.einsum("hts,hti->hsi", out_score, query_p, precision=highest)
        grad_k = grad_k + jnp.einsum("hsj,hij->hsi", values_p, state, precision=highest)
        grad_v = jnp.einsum("hts,htj->hsj", key_score, grad_p, precision=highest)
        grad_v = grad_v + jnp.einsum("hsi,hij->hsj", keys_p, state, precision=highest)
        state = state + jnp.einsum("hti,htj->hij", query_p, grad_p, precision=highest)
        return state, (grad_k, grad_v)

    pieces = (query_b, keys_b, values_b, grad_b)
    unused, grad_q = lax.scan(forward, empty_state, pieces)
    unused, (grad_k, grad_v) = lax.scan(backward, empty_state, pieces, reverse=True)

    def merge(array):
        return array.transpose(0, 2, 1, 3).reshape(SEQLEN, HEADS * HD).astype(jnp.bfloat16)

    return merge(grad_q), merge(grad_k), merge(grad_v)
```

```python
import functools

import jax
import jax.numpy as jnp
from jax import lax
from jax.experimental import pallas as pl
from jax.experimental.pallas import tpu as pltpu
from jax.sharding import PartitionSpec as P

HD = 128
CHUNKS = 8
X_LAG = 1
CORE_LAG = 1
MESH = pl.DeviceIdType.MESH
F32 = jnp.float32
BF16 = jnp.bfloat16


def dot(a, b, ca, cb):
    return lax.dot_general(a, b, (((ca,), (cb,)), ((), ())), preferred_element_type=F32)


def columns(head):
    return pl.ds(pl.multiple_of(head * HD, HD), HD)


def kernel(
    count, half, q_ref, k_ref, v_ref, g_ref, oq_ref, ok_ref, ov_ref,
    own, t_out, t_in, c_out, c_in, x_out, x_in, mine, f_out, f_in,
    t_ss, t_rs, c_ss, c_rs, x_ss, x_rs, f_ss, f_rs,
):
    per = half // CHUNKS
    z = lax.axis_index("seq")
    h = lax.axis_index("head")
    hx, hc = h // 2, h % 2
    core_peer = hx * 2 + (1 - hc)
    x_peer = (1 - hx) * 2 + hc
    my_first = hc * half
    peer_first = (1 - hc) * half
    places = (z, count - 1 - z)
    nexts = (z + 1, z - 1)
    x_after = (hx, 1 - hx)
    core_after = (hc, 1 - hc)

    barrier = pltpu.get_barrier_semaphore()
    pl.semaphore_signal(barrier, inc=1, device_id={"head": core_peer}, device_id_type=MESH)
    pl.semaphore_signal(barrier, inc=1, device_id={"head": x_peer}, device_id_type=MESH)

    @pl.when(z > 0)
    def _():
        pl.semaphore_signal(barrier, inc=1, device_id={"seq": z - 1}, device_id_type=MESH)

    @pl.when(z < count - 1)
    def _():
        pl.semaphore_signal(barrier, inc=1, device_id={"seq": z + 1}, device_id_type=MESH)

    def remote(src, dst, ss, rs, lane, c, target):
        part = (lane, pl.ds(c * per, per))
        return pltpu.make_async_remote_copy(
            src_ref=src.at[part], dst_ref=dst.at[part],
            send_sem=ss.at[lane, c], recv_sem=rs.at[lane, c],
            device_id=target, device_id_type=MESH,
        )

    def t_copy(lane, c):
        return remote(t_out, t_in, t_ss, t_rs, lane, c, {"head": core_peer})

    def c_copy(lane, c):
        return remote(c_out, c_in, c_ss, c_rs, lane, c, {"seq": nexts[lane]})

    def x_copy(lane, c):
        return remote(x_out, x_in, x_ss, x_rs, lane, c, {"head": x_peer})

    def f_copy(lane, c):
        return remote(f_out, f_in, f_ss, f_rs, lane, c, {"head": core_peer})

    for lane in range(2):
        @pl.when(places[lane] == 0)
        def _():
            c_in[lane] = jnp.zeros(c_in.shape[1:], F32)

    def local_states(first, c, into):
        for i in range(per):
            j = c * per + i
            cols = columns(first + j)
            into[0, j] = dot(k_ref[:, cols], v_ref[:, cols], 0, 0)
            into[1, j] = dot(q_ref[:, cols], g_ref[:, cols], 0, 0)

    local_states(peer_first, 0, t_out)
    neighbours = 2 + jnp.where(z > 0, 1, 0) + jnp.where(z < count - 1, 1, 0)
    pl.semaphore_wait(barrier, neighbours)
    t_copy(0, 0).start()
    t_copy(1, 0).start()
    local_states(my_first, 0, own)

    def begin(c, carry):
        local_states(peer_first, c, t_out)
        t_copy(0, c).start()
        t_copy(1, c).start()
        local_states(my_first, c, own)
        return carry

    lax.fori_loop(1, CHUNKS, begin, 0)

    def chain(lane, c):
        place = places[lane]
        t_copy(lane, c).wait_recv()

        @pl.when(place > 0)
        def _():
            c_copy(lane, c).wait_recv()

        keep = (1 - x_after[lane]).astype(F32)
        for i in range(per):
            j = c * per + i
            total = own[lane, j] + t_in[lane, j]
            before = c_in[lane, j]
            c_out[lane, j] = before + total
            x_out[lane, j] = (before + keep * total).astype(BF16)

        @pl.when(place < count - 1)
        def _():
            c_copy(lane, c).start()

        x_copy(lane, c).start()

    def across(lane, c):
        x_copy(lane, c).wait_recv()
        after = core_after[lane].astype(F32)
        for i in range(per):
            j = c * per + i
            base = c_in[lane, j] + x_in[lane, j].astype(F32)
            f_out[lane, j] = base + (1.0 - after) * own[lane, j]
            mine[lane, j] = base + after * t_in[lane, j]
        f_copy(lane, c).start()

    rows = lax.broadcasted_iota(jnp.int32, (HD, HD), 0)
    cols_ = lax.broadcasted_iota(jnp.int32, (HD, HD), 1)

    def halves(state):
        high = state.astype(BF16)
        return high, (state - high.astype(F32)).astype(BF16)

    def finish_query(head, state):
        cols = columns(head)
        k, v, g = k_ref[:, cols], v_ref[:, cols], g_ref[:, cols]
        score = jnp.where(rows >= cols_, dot(g, v, 1, 1), 0.0).astype(BF16)
        high, low = halves(state)
        out = dot(score, k, 1, 0)
        out += dot(g, high, 1, 1) + dot(g, low, 1, 1)
        oq_ref[:, cols] = out.astype(BF16)

    def finish_pair(head, state):
        cols = columns(head)
        q, k, v, g = q_ref[:, cols], k_ref[:, cols], v_ref[:, cols], g_ref[:, cols]
        out_score = jnp.where(cols_ >= rows, dot(v, g, 1, 1), 0.0).astype(BF16)
        key_score = jnp.where(cols_ >= rows, dot(k, q, 1, 1), 0.0).astype(BF16)
        high, low = halves(state)
        gk = dot(out_score, q, 1, 0) + (dot(v, high, 1, 1) + dot(v, low, 1, 1))
        ok_ref[:, cols] = gk.astype(BF16)
        gv = dot(key_score, g, 1, 0) + (dot(k, high, 1, 0) + dot(k, low, 1, 0))
        ov_ref[:, cols] = gv.astype(BF16)

    finishes = (finish_query, finish_pair)

    def finish(lane, c):
        f_copy(lane, c).wait_recv()
        for i in range(per):
            j = c * per + i
            finishes[lane](my_first + j, mine[lane, j])
            finishes[lane](peer_first + j, f_in[lane, j])

    def step(t, carry):
        for lag, work in ((0, chain), (X_LAG, across), (X_LAG + CORE_LAG, finish)):
            for lane in range(2):
                c = t - lag - places[lane]

                @pl.when(jnp.logical_and(c >= 0, c < CHUNKS))
                def _():
                    work(lane, c)
        return carry

    lax.fori_loop(0, CHUNKS + count - 1 + X_LAG + CORE_LAG, step, 0)

    def drain(c, carry):
        for lane in range(2):
            t_copy(lane, c).wait_send()
            x_copy(lane, c).wait_send()
            f_copy(lane, c).wait_send()

            @pl.when(places[lane] < count - 1)
            def _():
                c_copy(lane, c).wait_send()
        return carry

    lax.fori_loop(0, CHUNKS, drain, 0)


def body(count, query, keys, values, grad_out):
    half = query.shape[1] // HD // 2
    state = pltpu.VMEM((2, half, HD, HD), F32)
    small = pltpu.VMEM((2, half, HD, HD), BF16)
    sems = pltpu.SemaphoreType.DMA((2, CHUNKS))
    vmem = pl.BlockSpec(memory_space=pltpu.VMEM)
    return pl.pallas_call(
        functools.partial(kernel, count, half),
        out_shape=(jax.ShapeDtypeStruct(query.shape, query.dtype),) * 3,
        in_specs=[vmem] * 4,
        out_specs=(vmem,) * 3,
        scratch_shapes=[state, state, state, state, state, small, small, state, state, state] + [sems] * 8,
        compiler_params=pltpu.CompilerParams(
            collective_id=0, has_side_effects=True, vmem_limit_bytes=48 * 1024 * 1024
        ),
        cost_estimate=pl.CostEstimate(flops=2 * 10**9, bytes_accessed=7 * 2**20, transcendentals=0),
    )(query, keys, values, grad_out)


def solution(mesh):
    spec = P(("rep", "seq", "head"), None)
    return jax.shard_map(
        functools.partial(body, mesh.shape["seq"]),
        mesh=mesh,
        in_specs=(spec,) * 4,
        out_specs=(spec,) * 3,
        check_vma=False,
    )
```

```python
import functools

import jax
import jax.numpy as jnp
from jax import lax
from jax.experimental import pallas as pl
from jax.experimental.pallas import tpu as pltpu
from jax.sharding import PartitionSpec as P

HD = 128
CHUNKS = 8
HOP = 2
X_LAG = 2
CORE_LAG = 1
MESH = pl.DeviceIdType.MESH
F32 = jnp.float32
BF16 = jnp.bfloat16


def dot(a, b, ca, cb):
    return lax.dot_general(a, b, (((ca,), (cb,)), ((), ())), preferred_element_type=F32)


def columns(head):
    return pl.ds(pl.multiple_of(head * HD, HD), HD)


def kernel(
    count, half, q_hbm, k_hbm, v_hbm, g_hbm, oq_ref, ok_ref, ov_ref,
    q_ref, k_ref, v_ref, g_ref,
    own, t_out, t_in, c_out, c_in, n_out, n_in, x_out, x_in, mine, f_out, f_in,
    t_ss, t_rs, c_ss, c_rs, x_ss, x_rs, f_ss, f_rs, in_sem,
):
    per = half // CHUNKS
    z = lax.axis_index("seq")
    h = lax.axis_index("head")
    hx, hc = h // 2, h % 2
    core_peer = hx * 2 + (1 - hc)
    x_peer = (1 - hx) * 2 + hc
    my_first = hc * half
    peer_first = (1 - hc) * half
    places = (z, count - 1 - z)
    nexts = (z + 1, z - 1)
    x_after = (hx, 1 - hx)
    core_after = (hc, 1 - hc)

    def load(side, n):
        src = (q_hbm, k_hbm, v_hbm, g_hbm)[n]
        dst = (q_ref, k_ref, v_ref, g_ref)[n]
        first = (peer_first, my_first)[side]
        cols = pl.ds(pl.multiple_of(first * HD, HD), half * HD)
        return pltpu.make_async_copy(src.at[:, cols], dst.at[:, cols], in_sem.at[side, n])

    for side in range(2):
        for n in range(4):
            load(side, n).start()

    barrier = pltpu.get_barrier_semaphore()
    pl.semaphore_signal(barrier, inc=1, device_id={"head": core_peer}, device_id_type=MESH)
    pl.semaphore_signal(barrier, inc=1, device_id={"head": x_peer}, device_id_type=MESH)

    @pl.when(z > 0)
    def _():
        pl.semaphore_signal(barrier, inc=1, device_id={"seq": z - 1}, device_id_type=MESH)

    @pl.when(z < count - 1)
    def _():
        pl.semaphore_signal(barrier, inc=1, device_id={"seq": z + 1}, device_id_type=MESH)

    def remote(src, dst, ss, rs, lane, c, target):
        part = (lane, pl.ds(c * per, per))
        return pltpu.make_async_remote_copy(
            src_ref=src.at[part], dst_ref=dst.at[part],
            send_sem=ss.at[lane, c], recv_sem=rs.at[lane, c],
            device_id=target, device_id_type=MESH,
        )

    def t_copy(lane, c):
        return remote(t_out, t_in, t_ss, t_rs, lane, c, {"head": core_peer})

    def c_copy(lane, c):
        return remote(c_out, c_in, c_ss, c_rs, lane, c, {"seq": nexts[lane]})

    def n_copy(lane, c):
        return remote(n_out, n_in, c_ss, c_rs, lane, c, {"seq": nexts[lane]})

    def x_copy(lane, c):
        return remote(x_out, x_in, x_ss, x_rs, lane, c, {"head": x_peer})

    def f_copy(lane, c):
        return remote(f_out, f_in, f_ss, f_rs, lane, c, {"head": core_peer})

    for lane in range(2):
        @pl.when(places[lane] == 0)
        def _():
            c_in[lane] = jnp.zeros(c_in.shape[1:], F32)
            n_in[lane] = jnp.zeros(n_in.shape[1:], BF16)

    def local_states(first, c, into):
        for i in range(per):
            j = c * per + i
            cols = columns(first + j)
            into[0, j] = dot(v_ref[:, cols], k_ref[:, cols], 0, 0)
            into[1, j] = dot(q_ref[:, cols], g_ref[:, cols], 0, 0)

    for n in range(4):
        load(0, n).wait()
    local_states(peer_first, 0, t_out)
    neighbours = 2 + jnp.where(z > 0, 1, 0) + jnp.where(z < count - 1, 1, 0)
    pl.semaphore_wait(barrier, neighbours)
    t_copy(0, 0).start()
    t_copy(1, 0).start()
    for n in range(4):
        load(1, n).wait()
    local_states(my_first, 0, own)

    def begin(c, carry):
        local_states(peer_first, c, t_out)
        t_copy(0, c).start()
        t_copy(1, c).start()
        local_states(my_first, c, own)
        return carry

    lax.fori_loop(1, CHUNKS, begin, 0)

    def chain(lane, c):
        place = places[lane]
        keep = (1 - x_after[lane]).astype(F32)
        t_copy(lane, c).wait_recv()

        def forward(copy, arrived, leaving, wide):
            @pl.when(place > 0)
            def _():
                copy(lane, c).wait_recv()

            for i in range(per):
                j = c * per + i
                total = own[lane, j] + t_in[lane, j]
                before = arrived[lane, j].astype(F32)
                if not wide:
                    c_in[lane, j] = before
                leaving[lane, j] = (before + total).astype(leaving.dtype)
                x_out[lane, j] = (before + keep * total).astype(BF16)

            @pl.when(place < count - 1)
            def _():
                copy(lane, c).start()

        @pl.when(c % 2 == 0)
        def _():
            forward(c_copy, c_in, c_out, True)

        @pl.when(c % 2 == 1)
        def _():
            forward(n_copy, n_in, n_out, False)

        x_copy(lane, c).start()

    def across(lane, c):
        x_copy(lane, c).wait_recv()
        after = core_after[lane].astype(F32)
        for i in range(per):
            j = c * per + i
            base = c_in[lane, j] + x_in[lane, j].astype(F32)
            f_out[lane, j] = base + (1.0 - after) * own[lane, j]
            mine[lane, j] = base + after * t_in[lane, j]
        f_copy(lane, c).start()

    rows = lax.broadcasted_iota(jnp.int32, (HD, HD), 0)
    cols_ = lax.broadcasted_iota(jnp.int32, (HD, HD), 1)

    def halves(state):
        high = state.astype(BF16)
        return high, (state - high.astype(F32)).astype(BF16)

    def finish_query(head, state):
        cols = columns(head)
        k, v, g = k_ref[:, cols], v_ref[:, cols], g_ref[:, cols]
        score = jnp.where(rows >= cols_, dot(g, v, 1, 1), 0.0).astype(BF16)
        high, low = halves(state)
        out = dot(jnp.concatenate([score, g, g], 1), jnp.concatenate([k, high, low], 0), 1, 0)
        oq_ref[:, cols] = out.astype(BF16)

    def finish_pair(head, state):
        cols = columns(head)
        q, k, v, g = q_ref[:, cols], k_ref[:, cols], v_ref[:, cols], g_ref[:, cols]
        out_score = jnp.where(cols_ >= rows, dot(v, g, 1, 1), 0.0).astype(BF16)
        key_score = jnp.where(cols_ >= rows, dot(k, q, 1, 1), 0.0).astype(BF16)
        high, low = halves(state)
        gk = dot(out_score, q, 1, 0)
        gk += dot(jnp.concatenate([v, v], 1), jnp.concatenate([high, low], 1), 1, 1)
        ok_ref[:, cols] = gk.astype(BF16)
        gv = dot(
            jnp.concatenate([key_score, k, k], 1), jnp.concatenate([g, high, low], 0), 1, 0
        )
        ov_ref[:, cols] = gv.astype(BF16)

    finishes = (finish_query, finish_pair)

    def finish(lane, c):
        f_copy(lane, c).wait_recv()
        for i in range(per):
            j = c * per + i
            finishes[lane](my_first + j, mine[lane, j])
            finishes[lane](peer_first + j, f_in[lane, j])

    def step(t, carry):
        for lag, work in ((0, chain), (X_LAG, across), (X_LAG + CORE_LAG, finish)):
            for lane in range(2):
                c = t - lag - HOP * places[lane]

                @pl.when(jnp.logical_and(c >= 0, c < CHUNKS))
                def _():
                    work(lane, c)
        return carry

    lax.fori_loop(0, CHUNKS + HOP * (count - 1) + X_LAG + CORE_LAG, step, 0)

    def drain(c, carry):
        for lane in range(2):
            t_copy(lane, c).wait_send()
            x_copy(lane, c).wait_send()
            f_copy(lane, c).wait_send()

            inner = places[lane] < count - 1

            @pl.when(jnp.logical_and(inner, c % 2 == 0))
            def _():
                c_copy(lane, c).wait_send()

            @pl.when(jnp.logical_and(inner, c % 2 == 1))
            def _():
                n_copy(lane, c).wait_send()
        return carry

    lax.fori_loop(0, CHUNKS, drain, 0)


def body(count, query, keys, values, grad_out):
    half = query.shape[1] // HD // 2
    state = pltpu.VMEM((2, half, HD, HD), F32)
    small = pltpu.VMEM((2, half, HD, HD), BF16)
    sems = pltpu.SemaphoreType.DMA((2, CHUNKS))
    vmem = pl.BlockSpec(memory_space=pltpu.VMEM)
    return pl.pallas_call(
        functools.partial(kernel, count, half),
        out_shape=(jax.ShapeDtypeStruct(query.shape, query.dtype),) * 3,
        in_specs=[pl.BlockSpec(memory_space=pl.ANY)] * 4,
        out_specs=(vmem,) * 3,
        scratch_shapes=[pltpu.VMEM(query.shape, query.dtype)] * 4
        + [state, state, state, state, state, small, small, small, small, state, state, state] + [sems] * 8
        + [pltpu.SemaphoreType.DMA((2, 4))],
        compiler_params=pltpu.CompilerParams(
            collective_id=0, has_side_effects=True, vmem_limit_bytes=48 * 1024 * 1024
        ),
        cost_estimate=pl.CostEstimate(flops=2 * 10**9, bytes_accessed=7 * 2**20, transcendentals=0),
    )(query, keys, values, grad_out)


def solution(mesh):
    spec = P(("rep", "seq", "head"), None)
    return jax.shard_map(
        functools.partial(body, mesh.shape["seq"]),
        mesh=mesh,
        in_specs=(spec,) * 4,
        out_specs=(spec,) * 3,
        check_vma=False,
    )
```

```python
import functools

import jax
import jax.numpy as jnp
from jax import lax
from jax.experimental import pallas as pl
from jax.experimental.pallas import tpu as pltpu
from jax.sharding import PartitionSpec as P

HD = 128
CHUNKS = 8
HOP = 2
X_LAG = 3
CORE_LAG = 1
MESH = pl.DeviceIdType.MESH
F32 = jnp.float32
BF16 = jnp.bfloat16


def dot(a, b, ca, cb):
    return lax.dot_general(a, b, (((ca,), (cb,)), ((), ())), preferred_element_type=F32)


def columns(head):
    return pl.ds(pl.multiple_of(head * HD, HD), HD)


def kernel(
    count, half, q_hbm, k_hbm, v_hbm, g_hbm, oq_ref, ok_ref, ov_ref,
    q_ref, k_ref, v_ref, g_ref,
    own, t_out, t_in, c_out, c_in, n_out, n_in, x_out, x_in, mine, f_out, f_in,
    t_ss, t_rs, c_ss, c_rs, x_ss, x_rs, f_ss, f_rs, in_sem,
):
    per = half // CHUNKS
    z = lax.axis_index("seq")
    h = lax.axis_index("head")
    hx, hc = h // 2, h % 2
    core_peer = hx * 2 + (1 - hc)
    x_peer = (1 - hx) * 2 + hc
    my_first = hc * half
    peer_first = (1 - hc) * half
    places = (z, count - 1 - z)
    nexts = (z + 1, z - 1)
    x_after = (hx, 1 - hx)
    core_after = (hc, 1 - hc)

    def load(side, n):
        src = (q_hbm, k_hbm, v_hbm, g_hbm)[n]
        dst = (q_ref, k_ref, v_ref, g_ref)[n]
        first = (peer_first, my_first)[side]
        cols = pl.ds(pl.multiple_of(first * HD, HD), half * HD)
        return pltpu.make_async_copy(src.at[:, cols], dst.at[:, cols], in_sem.at[side, n])

    for side in range(2):
        for n in range(4):
            load(side, n).start()

    barrier = pltpu.get_barrier_semaphore()
    pl.semaphore_signal(barrier, inc=1, device_id={"head": core_peer}, device_id_type=MESH)
    pl.semaphore_signal(barrier, inc=1, device_id={"head": x_peer}, device_id_type=MESH)

    @pl.when(z > 0)
    def _():
        pl.semaphore_signal(barrier, inc=1, device_id={"seq": z - 1}, device_id_type=MESH)

    @pl.when(z < count - 1)
    def _():
        pl.semaphore_signal(barrier, inc=1, device_id={"seq": z + 1}, device_id_type=MESH)

    def remote(src, dst, ss, rs, lane, c, target):
        part = (lane, pl.ds(c * per, per))
        return pltpu.make_async_remote_copy(
            src_ref=src.at[part], dst_ref=dst.at[part],
            send_sem=ss.at[lane, c], recv_sem=rs.at[lane, c],
            device_id=target, device_id_type=MESH,
        )

    def t_copy(lane, c):
        return remote(t_out, t_in, t_ss, t_rs, lane, c, {"head": core_peer})

    def c_copy(lane, c):
        return remote(c_out, c_in, c_ss, c_rs, lane, c, {"seq": nexts[lane]})

    def n_copy(lane, c):
        return remote(n_out, n_in, c_ss, c_rs, lane, c, {"seq": nexts[lane]})

    def x_copy(lane, c):
        return remote(x_out, x_in, x_ss, x_rs, lane, c, {"head": x_peer})

    def f_copy(lane, c):
        return remote(f_out, f_in, f_ss, f_rs, lane, c, {"head": core_peer})

    for lane in range(2):
        @pl.when(places[lane] == 0)
        def _():
            c_in[lane] = jnp.zeros(c_in.shape[1:], F32)
            n_in[lane] = jnp.zeros(n_in.shape[1:], BF16)

    def local_states(first, c, into):
        for i in range(per):
            j = c * per + i
            cols = columns(first + j)
            into[0, j] = dot(v_ref[:, cols], k_ref[:, cols], 0, 0)
            into[1, j] = dot(q_ref[:, cols], g_ref[:, cols], 0, 0)

    for n in range(4):
        load(0, n).wait()
    local_states(peer_first, 0, t_out)
    neighbours = 2 + jnp.where(z > 0, 1, 0) + jnp.where(z < count - 1, 1, 0)
    pl.semaphore_wait(barrier, neighbours)
    t_copy(0, 0).start()
    t_copy(1, 0).start()
    for n in range(4):
        load(1, n).wait()
    local_states(my_first, 0, own)

    def begin(c, carry):
        local_states(peer_first, c, t_out)
        t_copy(0, c).start()
        t_copy(1, c).start()
        local_states(my_first, c, own)
        return carry

    lax.fori_loop(1, CHUNKS, begin, 0)

    def chain(lane, c):
        place = places[lane]
        keep = (1 - x_after[lane]).astype(F32)
        t_copy(lane, c).wait_recv()

        def forward(copy, arrived, leaving, wide):
            @pl.when(place > 0)
            def _():
                copy(lane, c).wait_recv()

            for i in range(per):
                j = c * per + i
                total = own[lane, j] + t_in[lane, j]
                before = arrived[lane, j].astype(F32)
                if not wide:
                    c_in[lane, j] = before
                leaving[lane, j] = (before + total).astype(leaving.dtype)
                x_out[lane, j] = (before + keep * total).astype(BF16)

            @pl.when(place < count - 1)
            def _():
                copy(lane, c).start()

        @pl.when(c % 2 == 0)
        def _():
            forward(c_copy, c_in, c_out, True)

        @pl.when(c % 2 == 1)
        def _():
            forward(n_copy, n_in, n_out, False)

        x_copy(lane, c).start()

    def across(lane, c):
        x_copy(lane, c).wait_recv()
        after = core_after[lane].astype(F32)
        for i in range(per):
            j = c * per + i
            base = c_in[lane, j] + x_in[lane, j].astype(F32)
            f_out[lane, j] = base + (1.0 - after) * own[lane, j]
            mine[lane, j] = base + after * t_in[lane, j]
        f_copy(lane, c).start()

    rows = lax.broadcasted_iota(jnp.int32, (HD, HD), 0)
    cols_ = lax.broadcasted_iota(jnp.int32, (HD, HD), 1)

    def halves(state):
        high = state.astype(BF16)
        return high, (state - high.astype(F32)).astype(BF16)

    def finish_query(head, state):
        cols = columns(head)
        k, v, g = k_ref[:, cols], v_ref[:, cols], g_ref[:, cols]
        score = jnp.where(rows >= cols_, dot(g, v, 1, 1), 0.0).astype(BF16)
        high, low = halves(state)
        out = dot(jnp.concatenate([score, g, g], 1), jnp.concatenate([k, high, low], 0), 1, 0)
        oq_ref[:, cols] = out.astype(BF16)

    def finish_pair(head, state):
        cols = columns(head)
        q, k, v, g = q_ref[:, cols], k_ref[:, cols], v_ref[:, cols], g_ref[:, cols]
        out_score = jnp.where(cols_ >= rows, dot(v, g, 1, 1), 0.0).astype(BF16)
        key_score = jnp.where(cols_ >= rows, dot(k, q, 1, 1), 0.0).astype(BF16)
        high, low = halves(state)
        gk = dot(out_score, q, 1, 0)
        gk += dot(jnp.concatenate([v, v], 1), jnp.concatenate([high, low], 1), 1, 1)
        ok_ref[:, cols] = gk.astype(BF16)
        gv = dot(
            jnp.concatenate([key_score, k, k], 1), jnp.concatenate([g, high, low], 0), 1, 0
        )
        ov_ref[:, cols] = gv.astype(BF16)

    finishes = (finish_query, finish_pair)

    def finish(lane, c):
        f_copy(lane, c).wait_recv()
        for i in range(per):
            j = c * per + i
            finishes[lane](my_first + j, mine[lane, j])
            finishes[lane](peer_first + j, f_in[lane, j])

    def step(t, carry):
        for lag, work in ((0, chain), (X_LAG, across), (X_LAG + CORE_LAG, finish)):
            for lane in range(2):
                c = t - lag - HOP * places[lane]

                @pl.when(jnp.logical_and(c >= 0, c < CHUNKS))
                def _():
                    work(lane, c)
        return carry

    lax.fori_loop(0, CHUNKS + HOP * (count - 1) + X_LAG + CORE_LAG, step, 0)

    def drain(c, carry):
        for lane in range(2):
            t_copy(lane, c).wait_send()
            x_copy(lane, c).wait_send()
            f_copy(lane, c).wait_send()

            inner = places[lane] < count - 1

            @pl.when(jnp.logical_and(inner, c % 2 == 0))
            def _():
                c_copy(lane, c).wait_send()

            @pl.when(jnp.logical_and(inner, c % 2 == 1))
            def _():
                n_copy(lane, c).wait_send()
        return carry

    lax.fori_loop(0, CHUNKS, drain, 0)


def body(count, query, keys, values, grad_out):
    half = query.shape[1] // HD // 2
    state = pltpu.VMEM((2, half, HD, HD), F32)
    small = pltpu.VMEM((2, half, HD, HD), BF16)
    sems = pltpu.SemaphoreType.DMA((2, CHUNKS))
    vmem = pl.BlockSpec(memory_space=pltpu.VMEM)
    return pl.pallas_call(
        functools.partial(kernel, count, half),
        out_shape=(jax.ShapeDtypeStruct(query.shape, query.dtype),) * 3,
        in_specs=[pl.BlockSpec(memory_space=pl.ANY)] * 4,
        out_specs=(vmem,) * 3,
        scratch_shapes=[pltpu.VMEM(query.shape, query.dtype)] * 4
        + [state, state, state, state, state, small, small, small, small, state, state, state] + [sems] * 8
        + [pltpu.SemaphoreType.DMA((2, 4))],
        compiler_params=pltpu.CompilerParams(
            collective_id=0, has_side_effects=True, vmem_limit_bytes=48 * 1024 * 1024
        ),
        cost_estimate=pl.CostEstimate(flops=2 * 10**9, bytes_accessed=7 * 2**20, transcendentals=0),
    )(query, keys, values, grad_out)


def solution(mesh):
    spec = P(("rep", "seq", "head"), None)
    return jax.shard_map(
        functools.partial(body, mesh.shape["seq"]),
        mesh=mesh,
        in_specs=(spec,) * 4,
        out_specs=(spec,) * 3,
        check_vma=False,
    )
```
